256 devices in a mesh: mem: 64 (over y, z, core), sub: 4 (over x).
Axes of the slice: x: 4, y: 4, z: 8, core: 2. Of those that a mesh axis runs over, the one named last changes fastest.
Arguments:
- prior_realizations: float32 [128, 1024, 1024], P('mem', 'sub'), may hold values from -0.6 to 0.6
- soaked_part_table: float32 [128], P('mem'), may hold values from 0.15 to 0.6
- sightline_crossed_boxes: int32 [4, 64, 32], P('sub'), may hold values from 0 to 262143
- sightline_step_amount: int32 [4, 64], P('sub'), may hold values from 1 to 32, as said below
- camera_tile_displacement: int32 [4, 64, 128], P('sub'), may hold values from 0 to 4095
- camera_kelvin_data: float32 [4, 64, 128], P('sub', 'mem'), may hold values from -2 to 2
- camera_reciprocal_spread: float32 [4, 64, 128], P('sub', 'mem'), may hold values from 0.25 to 2
Outputs:
- analysis: float32 [128, 1024, 1024], P('mem', 'sub')
The draws below stay inside these ranges and needn't reach their ends.
Inputs may be any that keep to these rules, and one draw needn't show every extreme that they name: `sightline_step_amount`: every subdomain has a ray of 32 cells. `sightline_crossed_boxes`: row-major cell of the subdomain's 256 x 1024 block. `camera_tile_displacement`: cell within brick j of subdomain s.
All inputs are finite; a program needn't handle non-finite values.
Results may differ from the reference program's by a relative error of at most 0.0003.
Values sent between devices are 32-bit elements; how exact they have to be, the bound alone decides.
A program may use at most 320 MiB of HBM per device.

```python
import math
import jax
import jax.numpy as jnp
from jax import lax

MEMBERSHIP_CARD = 128
CX = 256
PLATE_SPAN_NORTH = 1024
SENSED_PER_BLOCK = 128
RAYS = 64
SEG = 32
ITERS = 20
PLATE_SPAN_EAST = 1024
BRICK = 4096
N_MEM = 64
N_SUB = 4


def draw_sightline_step_amount(key, part):
    key = jax.random.fold_in(key, 1)
    counts = jax.random.randint(key, (N_SUB, RAYS), 1, SEG + 1, dtype=jnp.int32)
    return counts.at[:, 0].set(SEG)


def plant(values, own_key, least, largest):
    spot = [jax.random.randint(jax.random.fold_in(own_key, axis), (), 0, length) for axis, length in enumerate(values.shape)]
    main_axis = values.shape.index(max(values.shape))
    next_to = spot[:main_axis] + [(spot[main_axis] + 1) % values.shape[main_axis]] + spot[main_axis + 1:]
    return values.at[tuple(spot)].set(least).at[tuple(next_to)].set(largest)


def level_of(rng, extent, shards, smallest, largest):
    factor_of = 1.0
    for dim, parts in shards:
        draws = jax.random.uniform(jax.random.fold_in(jax.random.fold_in(rng, 6), dim), (parts,), jnp.float32, smallest / len(shards), largest / len(shards))
        factor_of = factor_of * jnp.repeat(jnp.exp(draws), extent[dim] // parts).reshape((-1,) + (1,) * (len(extent) - 1 - dim))
    return factor_of


def normal_values(key, extent, scale, reach, split=(), held_as=jnp.bfloat16):
    level = level_of(key, extent, split, -0.22, 0.18) if split else 1.0
    array = jax.random.normal(key, extent, jnp.float32) * scale * level
    return jnp.minimum(jnp.maximum(array, -reach), reach).astype(held_as)


def setup_inputs(seed: int = 0) -> dict:
    key_list = jax.random.split(jax.random.key(seed), 8)
    prior_realizations = normal_values(key_list[0], (MEMBERSHIP_CARD, PLATE_SPAN_EAST, PLATE_SPAN_NORTH), 0.1, 0.6, ((0, 64), (1, 4)), jnp.float32)
    soaked_part_table = jnp.clip(jnp.exp(math.log(0.6) - 1.3862944 * jax.random.uniform(key_list[1], (MEMBERSHIP_CARD,), jnp.float32) ** level_of(key_list[1], (MEMBERSHIP_CARD,), ((0, 64),), -0.2, 0.2)), 0.15, 0.6)
    sightline_crossed_boxes = plant(jax.random.randint(key_list[2], (N_SUB, RAYS, SEG), 0, CX * PLATE_SPAN_NORTH), jax.random.fold_in(key_list[2], 1), 0, (CX * PLATE_SPAN_NORTH) - 1).astype(jnp.int32)
    sightline_step_amount = draw_sightline_step_amount(jax.random.fold_in(key_list[7], 71), 0)
    camera_tile_displacement = plant(jax.random.randint(key_list[4], (N_SUB, N_MEM, SENSED_PER_BLOCK), 0, BRICK), jax.random.fold_in(key_list[4], 1), 0, BRICK - 1).astype(jnp.int32)
    camera_kelvin_data = normal_values(key_list[5], (N_SUB, N_MEM, SENSED_PER_BLOCK), 0.3, 2.0, ((0, 4), (1, 64)), jnp.float32)
    camera_reciprocal_spread = jnp.clip(jnp.exp(math.log(2.0) - 2.0794415 * jax.random.uniform(key_list[6], (N_SUB, N_MEM, SENSED_PER_BLOCK), jnp.float32) ** level_of(key_list[6], (N_SUB, N_MEM, SENSED_PER_BLOCK), ((0, 4), (1, 64)), -0.2, 0.2)), 0.25, 2.0)
    return {"prior_realizations": prior_realizations, "soaked_part_table": soaked_part_table, "sightline_crossed_boxes": sightline_crossed_boxes, "sightline_step_amount": sightline_step_amount, "camera_tile_displacement": camera_tile_displacement, "camera_kelvin_data": camera_kelvin_data, "camera_reciprocal_spread": camera_reciprocal_spread}


conduct = 0.2

def laplace(kelvin_mesh):
    padded = jnp.pad(kelvin_mesh, ((0, 0), (1, 1), (1, 1)))
    across = padded[:, 2:, 1:-1] + padded[:, :-2, 1:-1] - 2.0 * kelvin_mesh
    along_z = padded[:, 1:-1, 2:] + padded[:, 1:-1, :-2] - 2.0 * kelvin_mesh
    return across + along_z

def ensemble_weights(gram_sum, pull_sum):
    members = gram_sum.shape[0]
    identity = jnp.eye(members, dtype=jnp.float32)
    system = (members - 1.0) * identity + gram_sum
    norm_scale = jnp.sqrt(jnp.sum(system * system))

    def newton_body(index_step, carry_pair):
        upper_iter, lower_iter = carry_pair
        newton_step = 1.5 * identity - 0.5 * jnp.dot(lower_iter, upper_iter, precision=lax.Precision.HIGHEST)
        return (jnp.dot(upper_iter, newton_step, precision=lax.Precision.HIGHEST), jnp.dot(newton_step, lower_iter, precision=lax.Precision.HIGHEST))
    upper_iter, lower_iter = lax.fori_loop(0, ITERS, newton_body, (system / norm_scale, identity))
    inv_root = lower_iter / jnp.sqrt(norm_scale)
    mean_shift = jnp.dot(inv_root, jnp.dot(inv_root, pull_sum, precision=lax.Precision.HIGHEST), precision=lax.Precision.HIGHEST)
    return math.sqrt(members - 1.0) * inv_root + mean_shift[:, None]

def reference(prior_realizations, soaked_part_table, sightline_crossed_boxes, sightline_step_amount, camera_tile_displacement, camera_kelvin_data, camera_reciprocal_spread):
    seg_index = jnp.arange(SEG, dtype=jnp.int32)
    live_mask = (seg_index[None, None, :] < sightline_step_amount[:, :, None]).astype(jnp.float32)
    fade_rate = soaked_part_table[:, None] * (1.0 - soaked_part_table[:, None]) ** seg_index.astype(jnp.float32)[None, :]
    amount = fade_rate[:, None, None, :] * live_mask[None]
    flat_cells = (sightline_crossed_boxes + (jnp.arange(N_SUB, dtype=jnp.int32) * (CX * PLATE_SPAN_NORTH))[:, None, None]).reshape(-1)
    melting_power_feed = jnp.zeros((MEMBERSHIP_CARD, PLATE_SPAN_EAST * PLATE_SPAN_NORTH), jnp.float32).at[:, flat_cells].add(amount.reshape(MEMBERSHIP_CARD, -1))
    melting_power_feed = melting_power_feed.reshape(MEMBERSHIP_CARD, PLATE_SPAN_EAST, PLATE_SPAN_NORTH)
    kelvin_mesh = prior_realizations
    for count_step in range(2):
        kelvin_mesh = kelvin_mesh + conduct * laplace(kelvin_mesh) + melting_power_feed
    bricks = kelvin_mesh.reshape(MEMBERSHIP_CARD, N_SUB, N_MEM, BRICK)
    mean_field = lax.optimization_barrier(jnp.sum(bricks, axis=0)) / MEMBERSHIP_CARD
    pert_field = bricks - mean_field[None]
    seen_pert = jnp.take_along_axis(pert_field, camera_tile_displacement[None], axis=3)
    predicted_average = jnp.take_along_axis(mean_field, camera_tile_displacement, axis=2)
    discrepancy = camera_kelvin_data - predicted_average
    weighted = seen_pert * camera_reciprocal_spread[None]
    gram_sum = jnp.einsum('msjp,nsjp->mn', weighted, seen_pert, precision=lax.Precision.HIGHEST)
    pull_sum = jnp.einsum('msjp,sjp->m', weighted, discrepancy, precision=lax.Precision.HIGHEST)
    transform = ensemble_weights(gram_sum, pull_sum)
    analysed = mean_field[None] + jnp.einsum('mn,msjb->nsjb', transform, pert_field, precision=lax.Precision.HIGHEST)
    return analysed.reshape(MEMBERSHIP_CARD, PLATE_SPAN_EAST, PLATE_SPAN_NORTH)
```

```python
import functools
import math

import jax
import jax.numpy as jnp
from jax import lax
from jax.experimental import pallas as pl
from jax.experimental.pallas import tpu as pltpu
from jax.sharding import PartitionSpec as P

MESH = pl.DeviceIdType.MESH
HIGHEST = lax.Precision.HIGHEST
ITERS = 20
CONDUCT = 0.2
F32, BF16, I32 = jnp.float32, jnp.bfloat16, jnp.int32
N_MEM, N_SUB = 64, 4
ROWS, COLS = 256, 1024
SEG, RAYS = 32, 64
PIX = 128
BLOCK = 32
STEP = 27
BATCHES = (12, 19, 26, 33, 40, 64)


def dot(a, b, precision=None):
    return jnp.dot(a, b, preferred_element_type=F32, precision=precision)


def iota(shape, dim):
    return lax.broadcasted_iota(I32, shape, dim)


def split(x):
    hi = x.astype(BF16)
    return hi, (x - hi.astype(F32)).astype(BF16)


def fades(share, shape):
    k = iota(shape, 1)
    base = jnp.broadcast_to(1.0 - share, shape)
    out = jnp.broadcast_to(share, shape)
    for bit in range(5):
        out = jnp.where(((k >> bit) & 1) == 1, out * base, out)
        base = base * base
    return out


def spread(v):
    col = iota(v.shape, 1)
    n = v.shape[0]
    left = jnp.where(col == 0, 0.0, pltpu.roll(v, 1, 1))
    right = jnp.where(col == COLS - 1, 0.0, pltpu.roll(v, COLS - 1, 1))
    return CONDUCT * (v + pltpu.roll(v, 1, 0) + pltpu.roll(v, n - 1, 0) + left + right)


def kernel(
    prior, share, cells, steps, pixel, kelvin, weight,
    out, extra,
    field, halo_s, halo_t, flown, onehot, amount_hi, amount_lo,
    pix, pix_in, gram_out, gram_in, part_in, full,
    got, got_hi, got_lo, grid_hi, grid_lo, back,
    load_sem, up_sem, down_sem, big_send, big_recv, pix_send, pix_recv,
    gram_send, gram_recv, part_send, part_recv, full_send, full_recv, back_send, back_recv,
):
    me, sub = lax.axis_index("mem"), lax.axis_index("sub")
    y, zc = me // 16, lax.rem(me, 16)
    q = y * N_SUB + sub

    def plane_peer(i):
        return lax.rem(me + i, N_MEM)

    def xy_peer(p):
        return ((p // N_SUB) * 16 + zc, lax.rem(p, N_SUB))

    def zc_peer(p):
        return (y * 16 + p, sub)

    above = (me, lax.rem(sub + N_SUB - 1, N_SUB))
    below = (me, lax.rem(sub + 1, N_SUB))

    barrier = pltpu.get_barrier_semaphore()

    @pl.loop(1, N_MEM)
    def _(i):
        pl.semaphore_signal(barrier, inc=1, device_id=(plane_peer(i), sub), device_id_type=MESH)

    @pl.loop(1, 16)
    def _(i):
        pl.semaphore_signal(barrier, inc=1, device_id=xy_peer(lax.rem(q + i, 16)), device_id_type=MESH)

    load = pltpu.make_async_copy(prior, field.at[:, pl.ds(8, ROWS)], load_sem)
    load.start()

    lanes = iota((RAYS, COLS), 1)
    upright = jnp.transpose(cells[...])
    for k in range(SEG):
        col = upright[:, k : k + 1] & (COLS - 1)
        onehot[k * RAYS : (k + 1) * RAYS, :] = jnp.where(lanes == col, 1.0, 0.0).astype(BF16)

    quad = [
        jnp.concatenate([cells[4 * c + i : 4 * c + i + 1, :] for i in range(4)], axis=1)
        for c in range(8)
    ]
    live_steps = jnp.concatenate([steps[...]] * 4, axis=1)

    def amounts(fade8):
        for c in range(8):
            step = iota((SEG, 256), 1) // RAYS + 4 * c
            grown = jnp.where(iota((SEG, 256), 0) == step, 1.0, 0.0)
            value = dot(fade8, grown, HIGHEST)
            value = jnp.where(step[:1] < live_steps, value, 0.0)
            hit = iota((ROWS, 256), 0) == (quad[c] >> 10)
            for m in range(2):
                row = value[m : m + 1, :]
                hi = row.astype(BF16).astype(F32)
                here = (slice(m * ROWS, (m + 1) * ROWS), slice(c * 256, (c + 1) * 256))
                amount_hi[here] = jnp.where(hit, hi, 0.0).astype(BF16)
                amount_lo[here] = jnp.where(hit, row - hi, 0.0).astype(BF16)

    def sources(into):
        @pl.loop(0, 4)
        def _(t):
            here = pl.ds(pl.multiple_of(t * 256, 256), 256)
            hot = onehot[:, here]
            total = dot(amount_hi[...], hot) + dot(amount_lo[...], hot)
            for m in range(2):
                into[m, pl.ds(8, ROWS), here] = total[m * ROWS : (m + 1) * ROWS]

    first = iota((8, SEG), 0)
    own = jnp.where(first == 0, share[0], share[1])
    amounts(fades(own, (8, SEG)))

    pl.semaphore_wait(barrier, N_MEM - 1 + 15)

    def halo_copies(ref, top, bottom, slot):
        return (
            pltpu.make_async_remote_copy(
                top, ref.at[:, pl.ds(ROWS + 8, 8)], up_sem.at[0, slot], up_sem.at[1, slot],
                device_id=above, device_id_type=MESH,
            ),
            pltpu.make_async_remote_copy(
                bottom, ref.at[:, pl.ds(0, 8)], down_sem.at[0, slot], down_sem.at[1, slot],
                device_id=below, device_id_type=MESH,
            ),
        )

    edges = halo_copies(field, prior.at[:, pl.ds(0, 8)], prior.at[:, pl.ds(ROWS - 8, 8)], 0)
    for copy in edges:
        copy.start()

    sources(halo_s)
    source_edges = halo_copies(halo_s, halo_s.at[:, pl.ds(8, 8)], halo_s.at[:, pl.ds(ROWS, 8)], 1)
    for copy in source_edges:
        copy.start()

    def inside(b, v):
        row = sub * ROWS + b * BLOCK - 8 + iota(v.shape, 0)
        return jnp.where((row >= 0) & (row < N_SUB * ROWS), v, 0.0)

    load.wait()
    for copy in edges:
        copy.wait()

    @pl.loop(0, ROWS // BLOCK)
    def _(b):
        start = pl.multiple_of(b * BLOCK, BLOCK)
        for m in range(2):
            v = inside(b, field[m, pl.ds(start, BLOCK + 16), :])
            v = spread(inside(b, spread(v)))
            flown[m, pl.ds(start, BLOCK), :] = v[8 : BLOCK + 8]

    def block_of(ref, d):
        return ref.at[
            :, pl.ds(pl.multiple_of((d // 2) * 8, 8), 8),
            pl.ds(pl.multiple_of(lax.rem(d, 2) * 512, 512), 512),
        ]

    keep = pltpu.make_async_copy(block_of(flown, me), got.at[:, me], big_recv)
    keep.start()

    def send_big(low, high):
        @pl.loop(low, high)
        def _(k):
            d = plane_peer(lax.rem(k * STEP, N_MEM))
            pltpu.make_async_remote_copy(
                block_of(flown, d), got.at[:, me], big_send, big_recv,
                device_id=(d, sub), device_id_type=MESH,
            ).start()

    send_big(1, BATCHES[0])

    for copy in source_edges:
        copy.wait()

    sides = iota((8, PIX), 0)

    @pl.loop(0, ROWS // BLOCK)
    def _(b):
        start = pl.multiple_of(b * BLOCK, BLOCK)
        forecast = []
        for m in range(2):
            s = inside(b, halo_s[m, pl.ds(start, BLOCK + 16), :])
            s = s + spread(s)
            forecast.append(flown[m, pl.ds(start, BLOCK), :] + s[8 : BLOCK + 8])
        for t in range(BLOCK // 8):
            j = b * (BLOCK // 4) + 2 * t
            cell = jnp.where(sides < 4, pixel[pl.ds(j, 1), :], pixel[pl.ds(j + 1, 1), :])
            lane, part, row = cell & 127, (cell >> 7) & 7, cell >> 10
            for m in range(2):
                tile = forecast[m][8 * t : 8 * t + 8]
                found = jnp.zeros((8, PIX), F32)
                for w in range(8):
                    picked = jnp.take_along_axis(tile[:, w * 128 : (w + 1) * 128], lane, axis=1)
                    found = jnp.where(part == w, picked, found)
                found = jnp.where((sides & 3) == row, found, 0.0)
                pix[j, m : m + 1, :] = jnp.sum(found[0:4], axis=0, keepdims=True)
                pix[j + 1, m : m + 1, :] = jnp.sum(found[4:8], axis=0, keepdims=True)

    @pl.loop(1, N_MEM)
    def _(i):
        d = plane_peer(i)
        pltpu.make_async_remote_copy(
            pix.at[d], pix_in.at[me], pix_send, pix_recv, device_id=(d, sub), device_id_type=MESH
        ).start()

    send_big(BATCHES[0], BATCHES[1])
    pix_in[me] = pix[me]

    def settle(view, sem):
        pltpu.make_async_copy(view, view, sem).wait()

    settle(pix_in.at[pl.ds(0, N_MEM - 1)], pix_recv)

    seen = jnp.concatenate([pix_in[:, 0, :], pix_in[:, 1, :]], axis=0)
    average = jnp.sum(seen, axis=0, keepdims=True) / (2 * N_MEM)
    seen = seen - average
    misfit = jnp.where(iota((PIX, PIX), 0) == 0, kelvin[...] - average, 0.0)
    both = jnp.concatenate([seen, misfit], axis=0)
    gram = lax.dot_general(
        seen * weight[...], both, (((1,), (1,)), ((), ())),
        preferred_element_type=F32, precision=HIGHEST,
    )
    row, col = iota((2 * N_MEM, 256), 0), iota((2 * N_MEM, 256), 1)
    carried = jnp.where(row == me, share[0], jnp.where(row == N_MEM + me, share[1], 0.0))
    gram = jnp.where((col == 129) & (sub == 0), carried, gram)
    gram_out[...] = gram.reshape(16, 8, 256)

    def to_peers(count_from, source, target, send, recv, peer):
        @pl.loop(1, 16)
        def _(i):
            p = lax.rem(count_from + i, 16)
            pltpu.make_async_remote_copy(
                source(p), target, send, recv, device_id=peer(p), device_id_type=MESH
            ).start()

    to_peers(q, lambda p: gram_out.at[p], gram_in.at[q], gram_send, gram_recv, xy_peer)
    send_big(BATCHES[1], BATCHES[2])
    gram_in[q] = gram_out[q]
    settle(gram_in.at[pl.ds(0, 15)], gram_recv)
    part_in[zc] = jnp.sum(gram_in[...], axis=0)
    to_peers(zc, lambda p: part_in.at[zc], part_in.at[zc], part_send, part_recv, zc_peer)
    send_big(BATCHES[2], BATCHES[3])
    settle(part_in.at[pl.ds(0, 15)], part_recv)
    full[q] = jnp.sum(part_in[...], axis=0)
    to_peers(q, lambda p: full.at[q], full.at[q], full_send, full_recv, xy_peer)
    send_big(BATCHES[3], BATCHES[4])
    settle(full.at[pl.ds(0, 15)], full_recv)
    send_big(BATCHES[4], BATCHES[5])

    n = 2 * N_MEM
    total = full[...].reshape(n, 256)
    eye = jnp.where(iota((n, n), 0) == iota((n, n), 1), 1.0, 0.0)
    system = (n - 1.0) * eye + total[:, :n]
    norm = jnp.sqrt(jnp.sum(system * system, axis=(0, 1), keepdims=True))

    def parts(x):
        a = x.astype(BF16)
        x = x - a.astype(F32)
        b = x.astype(BF16)
        return a, b, (x - b.astype(F32)).astype(BF16)

    def dot6(x, y):
        (a, b, c), (d, e, f) = x, y
        left = jnp.concatenate([a, a], axis=1), jnp.concatenate([b, a], axis=1), jnp.concatenate([c, b], axis=1)
        right = jnp.concatenate([d, e], axis=0), jnp.concatenate([d, f], axis=0)
        return dot(left[0], right[0]) + (dot(left[1], right[1]) + dot(left[2], right[0]))

    def newton(_, pair):
        u, v = parts(pair[0]), parts(pair[1])
        s = parts(1.5 * eye - 0.5 * dot6(v, u))
        return dot6(u, s), dot6(s, v)

    _, v = lax.fori_loop(0, ITERS, newton, (system / norm, eye))
    root = v / jnp.sqrt(norm)
    shift = dot(root, dot(root, total[:, n:], HIGHEST), HIGHEST)[:, :1]
    transform = math.sqrt(n - 1.0) * root + shift

    fade = fades(total[:, n + 1 : n + 2], (n, SEG))
    fade_mean = jnp.sum(fade, axis=0, keepdims=True) / n
    fade = fade - fade_mean
    mixed = []
    for m in range(2):
        column = jnp.where(iota((n, n), 1) == m * N_MEM + me, transform, 0.0)
        column = jnp.sum(column, axis=1, keepdims=True)
        mixed.append(fade_mean + jnp.sum(column * fade, axis=0, keepdims=True))

    grow = jnp.where(iota((n, 8 * n), 0) == iota((n, 8 * n), 1) // 8, 1.0, 0.0).astype(BF16)
    turned_hi, turned_lo = split(jnp.transpose(transform))
    grid_lo[...] = grow
    grid_hi[...] = dot(turned_hi, grid_lo[...]).astype(BF16)
    grid_lo[...] = dot(turned_lo, grid_lo[...]).astype(BF16)

    settle(got, big_recv)
    mean = jnp.sum(got[...], axis=(0, 1)) / n
    mean2 = jnp.concatenate([mean, mean], axis=0)

    @pl.loop(0, N_MEM)
    def _(i):
        m, s = i // (N_MEM // 2), lax.rem(i, N_MEM // 2)
        pert = got[m, pl.ds(2 * s, 2)].reshape(16, 512) - mean2
        hi, lo = split(pert)
        here = pl.ds(pl.multiple_of(i * 16, 16), 16)
        got_hi[here, :] = hi
        got_lo[here, :] = lo

    same_row = lax.rem(iota((n, 8 * n), 0), 8) == lax.rem(iota((n, 8 * n), 1), 8)

    @pl.loop(0, 8)
    def _(c):
        c = lax.rem(me // 8 + c, 8)
        r, k = iota((n, n), 0), iota((n, n), 1)
        pick = (r // N_MEM) * N_MEM + 8 * c + lax.rem(r, N_MEM) // 8 == k
        pick = jnp.where(pick, 1.0, 0.0).astype(BF16)
        hi = jnp.where(same_row, dot(pick, grid_hi[...]), 0.0).astype(BF16)
        lo = jnp.where(same_row, dot(pick, grid_lo[...]), 0.0).astype(BF16)
        new = dot(hi, got_hi[...]) + (dot(hi, got_lo[...]) + dot(lo, got_hi[...]))
        new = new.reshape(2, 8, 8, 512) + mean
        back[:, pl.ds(8 * c, 8)] = new

        @pl.loop(0, 8)
        def _(i):
            d = 8 * c + lax.rem(me + i, 8)

            @pl.when(d == me)
            def _():
                pltpu.make_async_copy(back.at[:, d], block_of(out, me), back_recv).start()

            @pl.when(d != me)
            def _():
                pltpu.make_async_remote_copy(
                    back.at[:, d], block_of(out, me), back_send, back_recv,
                    device_id=(d, sub), device_id_type=MESH,
                ).start()

    amounts(jnp.where(first == 0, mixed[0], jnp.where(first == 1, mixed[1], 0.0)))
    sources(halo_t)
    mixed_edges = halo_copies(halo_t, halo_t.at[:, pl.ds(8, 8)], halo_t.at[:, pl.ds(ROWS, 8)], 2)
    for copy in mixed_edges:
        copy.start()
    for copy in mixed_edges:
        copy.wait()

    @pl.loop(0, ROWS // BLOCK)
    def _(b):
        start = pl.multiple_of(b * BLOCK, BLOCK)
        for m in range(2):
            s = inside(b, halo_t[m, pl.ds(start, BLOCK + 16), :])
            s = s + spread(s)
            extra[m, pl.ds(start, BLOCK), :] = s[8 : BLOCK + 8]

    settle(got.at[:, pl.ds(0, N_MEM - 1)], big_send)
    settle(pix.at[pl.ds(0, N_MEM - 1)], pix_send)
    settle(gram_out.at[pl.ds(0, 15)], gram_send)
    settle(part_in.at[pl.ds(0, 15)], part_send)
    settle(full.at[pl.ds(0, 15)], full_send)
    settle(back.at[:, pl.ds(0, N_MEM - 1)], back_send)
    settle(out, back_recv)


def body(prior, share, cells, steps, pixel, kelvin, weight):
    vmem, any_space = pl.BlockSpec(memory_space=pltpu.VMEM), pl.BlockSpec(memory_space=pl.ANY)
    dma = pltpu.SemaphoreType.DMA
    shape = jax.ShapeDtypeStruct((2, ROWS, COLS), F32)
    n = 2 * N_MEM
    returned, extra = pl.pallas_call(
        kernel,
        out_shape=(shape, shape),
        in_specs=[any_space, pl.BlockSpec(memory_space=pltpu.SMEM)] + [vmem] * 5,
        out_specs=(any_space, vmem),
        scratch_shapes=[
            pltpu.VMEM((2, ROWS + 16, COLS), F32),
            pltpu.VMEM((2, ROWS + 16, COLS), F32),
            pltpu.VMEM((2, ROWS + 16, COLS), F32),
            pltpu.VMEM((2, ROWS, COLS), F32),
            pltpu.VMEM((SEG * RAYS, COLS), BF16),
            pltpu.VMEM((2 * ROWS, SEG * RAYS), BF16),
            pltpu.VMEM((2 * ROWS, SEG * RAYS), BF16),
            pltpu.VMEM((N_MEM, 2, PIX), F32),
            pltpu.VMEM((N_MEM, 2, PIX), F32),
            pltpu.VMEM((16, 8, 256), F32),
            pltpu.VMEM((16, 8, 256), F32),
            pltpu.VMEM((16, 8, 256), F32),
            pltpu.VMEM((16, 8, 256), F32),
            pltpu.VMEM((2, N_MEM, 8, 512), F32),
            pltpu.VMEM((8 * n, 512), BF16),
            pltpu.VMEM((8 * n, 512), BF16),
            pltpu.VMEM((n, 8 * n), BF16),
            pltpu.VMEM((n, 8 * n), BF16),
            pltpu.VMEM((2, N_MEM, 8, 512), F32),
            dma,
            dma((2, 3)),
            dma((2, 3)),
        ]
        + [dma] * 12,
        compiler_params=pltpu.CompilerParams(
            collective_id=0, has_side_effects=True, vmem_limit_bytes=56 * 2**20
        ),
    )(prior, share, cells[0].T, steps, pixel[0], kelvin[0], weight[0])
    return returned + extra


def solution(mesh):
    placed = (
        P("mem", "sub", None),
        P("mem"),
        P("sub", None, None),
        P("sub", None),
        P("sub", None, None),
        P("sub", "mem", None),
        P("sub", "mem", None),
    )
    return jax.shard_map(
        body, mesh=mesh, in_specs=placed, out_specs=P("mem", "sub", None), check_vma=False
    )
```

```python
import functools
import math

import jax
import jax.numpy as jnp
from jax import lax
from jax.experimental import pallas as pl
from jax.experimental.pallas import tpu as pltpu
from jax.sharding import PartitionSpec as P

MESH = pl.DeviceIdType.MESH
HIGHEST = lax.Precision.HIGHEST
ITERS = 20
CONDUCT = 0.2
F32, BF16, I32 = jnp.float32, jnp.bfloat16, jnp.int32
N_MEM, N_SUB = 64, 4
ROWS, COLS = 256, 1024
SEG, RAYS = 32, 64
PIX = 128
BLOCK = 32
INNER = 24
STEP = 27
BATCHES = (24, 36, 38, 48, 56, 64)


def dot(a, b, precision=None):
    return jnp.dot(a, b, preferred_element_type=F32, precision=precision)


def iota(shape, dim):
    return lax.broadcasted_iota(I32, shape, dim)


def split(x):
    hi = x.astype(BF16)
    return hi, (x - hi.astype(F32)).astype(BF16)


def fades(share, shape):
    k = iota(shape, 1)
    base = jnp.broadcast_to(1.0 - share, shape)
    out = jnp.broadcast_to(share, shape)
    for bit in range(5):
        out = jnp.where(((k >> bit) & 1) == 1, out * base, out)
        base = base * base
    return out


def spread(v):
    col = iota(v.shape, 1)
    n = v.shape[0]
    left = jnp.where(col == 0, 0.0, pltpu.roll(v, 1, 1))
    right = jnp.where(col == COLS - 1, 0.0, pltpu.roll(v, COLS - 1, 1))
    return CONDUCT * (v + pltpu.roll(v, 1, 0) + pltpu.roll(v, n - 1, 0) + left + right)


def kernel(
    prior, share, cells_in, steps_in, pixel_in, kelvin_in, weight_in,
    out,
    extra, cells, steps, pixel, kelvin, weight, field, halo_s, halo_t, flown, onehot, amount,
    pix, pix_in, gram_out, gram_in, part_in, full,
    got, got_hi, got_lo, grid_hi, grid_lo, back,
    load_sem, small_sem, up_sem, down_sem, big_send, big_recv, pix_send, pix_recv,
    gram_send, gram_recv, part_send, part_recv, full_send, full_recv, back_send, back_recv,
):
    me, sub = lax.axis_index("mem"), lax.axis_index("sub")
    y, zc = me // 16, lax.rem(me, 16)
    q = y * N_SUB + sub

    def plane_peer(i):
        return lax.rem(me + i, N_MEM)

    def xy_peer(p):
        return ((p // N_SUB) * 16 + zc, lax.rem(p, N_SUB))

    def zc_peer(p):
        return (y * 16 + p, sub)

    above = (me, lax.rem(sub + N_SUB - 1, N_SUB))
    below = (me, lax.rem(sub + 1, N_SUB))

    barrier = pltpu.get_barrier_semaphore()

    @pl.loop(1, N_MEM)
    def _(i):
        pl.semaphore_signal(barrier, inc=1, device_id=(plane_peer(i), sub), device_id_type=MESH)

    @pl.loop(1, 16)
    def _(i):
        pl.semaphore_signal(barrier, inc=1, device_id=xy_peer(lax.rem(q + i, 16)), device_id_type=MESH)

    load = pltpu.make_async_copy(prior, field.at[:, pl.ds(8, ROWS)], load_sem)
    load.start()
    small = [
        pltpu.make_async_copy(source, target, small_sem.at[i])
        for i, (source, target) in enumerate((
            (cells_in, cells), (steps_in, steps), (pixel_in, pixel), (kelvin_in, kelvin), (weight_in, weight)
        ))
    ]
    for copy in small:
        copy.start()

    pl.semaphore_wait(barrier, N_MEM - 1 + 15)

    def halo_copies(ref, top, bottom, slot):
        return (
            pltpu.make_async_remote_copy(
                top, ref.at[:, pl.ds(ROWS + 8, 8)], up_sem.at[0, slot], up_sem.at[1, slot],
                device_id=above, device_id_type=MESH,
            ),
            pltpu.make_async_remote_copy(
                bottom, ref.at[:, pl.ds(0, 8)], down_sem.at[0, slot], down_sem.at[1, slot],
                device_id=below, device_id_type=MESH,
            ),
        )

    edges = halo_copies(field, prior.at[:, pl.ds(0, 8)], prior.at[:, pl.ds(ROWS - 8, 8)], 0)
    for copy in edges:
        copy.start()

    def inside(b, v):
        row = sub * ROWS + b * BLOCK - 8 + iota(v.shape, 0)
        return jnp.where((row >= 0) & (row < N_SUB * ROWS), v, 0.0)

    load.wait()

    @pl.loop(0, (ROWS - 16) // INNER)
    def _(b):
        start = pl.multiple_of(8 + b * INNER, 8)
        for m in range(2):
            v = spread(spread(field[m, pl.ds(start, INNER + 16), :]))
            flown[m, pl.ds(start, INNER), :] = v[8 : INNER + 8]

    def block_of(ref, d):
        return ref.at[
            :, pl.ds(pl.multiple_of((d // 2) * 8, 8), 8),
            pl.ds(pl.multiple_of(lax.rem(d, 2) * 512, 512), 512),
        ]

    def send_big(low, high):
        @pl.loop(low, high)
        def _(k):
            d = plane_peer(lax.rem(k * STEP, N_MEM))
            pltpu.make_async_remote_copy(
                block_of(flown, d), got.at[:, me], big_send, big_recv,
                device_id=(d, sub), device_id_type=MESH,
            ).start()

    for copy in edges:
        copy.wait()
    for start in (0, ROWS - 8):
        row = sub * ROWS + start - 8 + iota((24, COLS), 0)
        real = (row >= 0) & (row < N_SUB * ROWS)
        for m in range(2):
            v = jnp.where(real, field[m, start : start + 24, :], 0.0)
            v = spread(jnp.where(real, spread(v), 0.0))
            flown[m, start : start + 8, :] = v[8:16]

    keep = pltpu.make_async_copy(block_of(flown, me), got.at[:, me], big_recv)
    keep.start()
    send_big(1, BATCHES[0])

    for copy in small:
        copy.wait()

    lanes = iota((RAYS, COLS), 1)
    upright = jnp.transpose(cells[...])
    for k in range(SEG):
        col = upright[:, k : k + 1] & (COLS - 1)
        onehot[k * RAYS : (k + 1) * RAYS, :] = jnp.where(lanes == col, 1.0, 0.0).astype(BF16)

    quad = [
        jnp.concatenate([cells[4 * c + i : 4 * c + i + 1, :] for i in range(4)], axis=1)
        for c in range(8)
    ]
    live_steps = jnp.concatenate([steps[...]] * 4, axis=1)

    def amounts(fade8):
        for c in range(8):
            step = iota((SEG, 256), 1) // RAYS + 4 * c
            grown = jnp.where(iota((SEG, 256), 0) == step, 1.0, 0.0)
            value = dot(fade8, grown, HIGHEST)
            value = jnp.where(step[:1] < live_steps, value, 0.0)
            hit = iota((ROWS, 256), 0) == (quad[c] >> 10)
            for m in range(2):
                row = value[m : m + 1, :]
                hi = row.astype(BF16).astype(F32)
                for part, piece in enumerate((hi, row - hi)):
                    top = (2 * part + m) * ROWS
                    amount[top : top + ROWS, c * 256 : (c + 1) * 256] = jnp.where(
                        hit, piece, 0.0
                    ).astype(BF16)

    def sources(into):
        @pl.loop(0, 4)
        def _(t):
            here = pl.ds(pl.multiple_of(t * 256, 256), 256)
            total = dot(amount[...], onehot[:, here])
            total = total[: 2 * ROWS] + total[2 * ROWS :]
            for m in range(2):
                into[m, pl.ds(8, ROWS), here] = total[m * ROWS : (m + 1) * ROWS]

    first = iota((8, SEG), 0)
    own = jnp.where(first == 0, share[0], share[1])
    amounts(fades(own, (8, SEG)))

    sources(halo_s)
    source_edges = halo_copies(halo_s, halo_s.at[:, pl.ds(8, 8)], halo_s.at[:, pl.ds(ROWS, 8)], 1)
    for copy in source_edges:
        copy.start()

    for copy in source_edges:
        copy.wait()

    sides = iota((8, PIX), 0)

    @pl.loop(0, ROWS // BLOCK)
    def _(b):
        start = pl.multiple_of(b * BLOCK, BLOCK)
        forecast = []
        for m in range(2):
            s = inside(b, halo_s[m, pl.ds(start, BLOCK + 16), :])
            s = s + spread(s)
            forecast.append(flown[m, pl.ds(start, BLOCK), :] + s[8 : BLOCK + 8])
        for t in range(BLOCK // 8):
            j = b * (BLOCK // 4) + 2 * t
            cell = jnp.where(sides < 4, pixel[pl.ds(j, 1), :], pixel[pl.ds(j + 1, 1), :])
            lane, part, row = cell & 127, (cell >> 7) & 7, cell >> 10
            for m in range(2):
                tile = forecast[m][8 * t : 8 * t + 8]
                found = jnp.zeros((8, PIX), F32)
                for w in range(8):
                    picked = jnp.take_along_axis(tile[:, w * 128 : (w + 1) * 128], lane, axis=1)
                    found = jnp.where(part == w, picked, found)
                found = jnp.where((sides & 3) == row, found, 0.0)
                pix[j, m : m + 1, :] = jnp.sum(found[0:4], axis=0, keepdims=True)
                pix[j + 1, m : m + 1, :] = jnp.sum(found[4:8], axis=0, keepdims=True)

    @pl.loop(1, N_MEM)
    def _(i):
        d = plane_peer(i)
        pltpu.make_async_remote_copy(
            pix.at[d], pix_in.at[me], pix_send, pix_recv, device_id=(d, sub), device_id_type=MESH
        ).start()

    send_big(BATCHES[0], BATCHES[1])
    pix_in[me] = pix[me]

    def settle(view, sem):
        pltpu.make_async_copy(view, view, sem).wait()

    settle(pix_in.at[pl.ds(0, N_MEM - 1)], pix_recv)

    seen = jnp.concatenate([pix_in[:, 0, :], pix_in[:, 1, :]], axis=0)
    average = jnp.sum(seen, axis=0, keepdims=True) / (2 * N_MEM)
    seen = seen - average
    misfit = jnp.where(iota((PIX, PIX), 0) == 0, kelvin[...] - average, 0.0)
    both = jnp.concatenate([seen, misfit], axis=0)
    gram = lax.dot_general(
        seen * weight[...], both, (((1,), (1,)), ((), ())),
        preferred_element_type=F32, precision=HIGHEST,
    )
    row, col = iota((2 * N_MEM, 256), 0), iota((2 * N_MEM, 256), 1)
    carried = jnp.where(row == me, share[0], jnp.where(row == N_MEM + me, share[1], 0.0))
    gram = jnp.where((col == 129) & (sub == 0), carried, gram)
    gram_out[...] = gram.reshape(16, 8, 256)

    def to_peers(count_from, source, target, send, recv, peer):
        @pl.loop(1, 16)
        def _(i):
            p = lax.rem(count_from + i, 16)
            pltpu.make_async_remote_copy(
                source(p), target, send, recv, device_id=peer(p), device_id_type=MESH
            ).start()

    to_peers(q, lambda p: gram_out.at[p], gram_in.at[q], gram_send, gram_recv, xy_peer)
    send_big(BATCHES[1], BATCHES[2])
    gram_in[q] = gram_out[q]
    settle(gram_in.at[pl.ds(0, 15)], gram_recv)
    part_in[zc] = jnp.sum(gram_in[...], axis=0)
    to_peers(zc, lambda p: part_in.at[zc], part_in.at[zc], part_send, part_recv, zc_peer)
    send_big(BATCHES[2], BATCHES[3])
    settle(part_in.at[pl.ds(0, 15)], part_recv)
    full[q] = jnp.sum(part_in[...], axis=0)
    to_peers(q, lambda p: full.at[q], full.at[q], full_send, full_recv, xy_peer)
    send_big(BATCHES[3], BATCHES[4])
    settle(full.at[pl.ds(0, 15)], full_recv)
    send_big(BATCHES[4], BATCHES[5])

    n = 2 * N_MEM
    total = full[...].reshape(n, 256)
    eye = jnp.where(iota((n, n), 0) == iota((n, n), 1), 1.0, 0.0)
    system = (n - 1.0) * eye + total[:, :n]
    norm = jnp.sqrt(jnp.sum(system * system, axis=(0, 1), keepdims=True))

    def parts(x):
        a = x.astype(BF16)
        x = x - a.astype(F32)
        b = x.astype(BF16)
        return a, b, (x - b.astype(F32)).astype(BF16)

    def dot6(x, y):
        (a, b, c), (d, e, f) = x, y
        left = jnp.concatenate([a, a], axis=1), jnp.concatenate([b, a], axis=1), jnp.concatenate([c, b], axis=1)
        right = jnp.concatenate([d, e], axis=0), jnp.concatenate([d, f], axis=0)
        return dot(left[0], right[0]) + (dot(left[1], right[1]) + dot(left[2], right[0]))

    def newton(_, pair):
        u, v = parts(pair[0]), parts(pair[1])
        s = parts(1.5 * eye - 0.5 * dot6(v, u))
        return dot6(u, s), dot6(s, v)

    _, v = lax.fori_loop(0, ITERS, newton, (system / norm, eye))
    root = v / jnp.sqrt(norm)
    shift = dot(root, dot(root, total[:, n:], HIGHEST), HIGHEST)[:, :1]
    transform = math.sqrt(n - 1.0) * root + shift

    fade = fades(total[:, n + 1 : n + 2], (n, SEG))
    fade_mean = jnp.sum(fade, axis=0, keepdims=True) / n
    fade = fade - fade_mean
    mixed = []
    for m in range(2):
        column = jnp.where(iota((n, n), 1) == m * N_MEM + me, transform, 0.0)
        column = jnp.sum(column, axis=1, keepdims=True)
        mixed.append(fade_mean + jnp.sum(column * fade, axis=0, keepdims=True))

    grow = jnp.where(iota((n, 8 * n), 0) == iota((n, 8 * n), 1) // 8, 1.0, 0.0).astype(BF16)
    turned_hi, turned_lo = split(jnp.transpose(transform))
    grid_lo[...] = grow
    grid_hi[...] = dot(turned_hi, grid_lo[...]).astype(BF16)
    grid_lo[...] = dot(turned_lo, grid_lo[...]).astype(BF16)

    settle(got, big_recv)
    mean = jnp.sum(got[...], axis=(0, 1)) / n
    mean2 = jnp.concatenate([mean, mean], axis=0)

    @pl.loop(0, N_MEM)
    def _(i):
        m, s = i // (N_MEM // 2), lax.rem(i, N_MEM // 2)
        pert = got[m, pl.ds(2 * s, 2)].reshape(16, 512) - mean2
        hi, lo = split(pert)
        here = pl.ds(pl.multiple_of(i * 16, 16), 16)
        got_hi[here, :] = hi
        got_lo[here, :] = lo

    same_row = lax.rem(iota((n, 8 * n), 0), 8) == lax.rem(iota((n, 8 * n), 1), 8)

    @pl.loop(0, 8)
    def _(c):
        c = lax.rem(me // 8 + c, 8)
        r, k = iota((n, n), 0), iota((n, n), 1)
        pick = (r // N_MEM) * N_MEM + 8 * c + lax.rem(r, N_MEM) // 8 == k
        pick = jnp.where(pick, 1.0, 0.0).astype(BF16)
        hi = jnp.where(same_row, dot(pick, grid_hi[...]), 0.0).astype(BF16)
        lo = jnp.where(same_row, dot(pick, grid_lo[...]), 0.0).astype(BF16)
        new = dot(hi, got_hi[...]) + (dot(hi, got_lo[...]) + dot(lo, got_hi[...]))
        new = new.reshape(2, 8, 8, 512) + mean
        back[:, pl.ds(8 * c, 8)] = new

        @pl.loop(0, 8)
        def _(i):
            d = 8 * c + lax.rem(me + i, 8)

            @pl.when(d == me)
            def _():
                pltpu.make_async_copy(back.at[:, d], block_of(out, me), back_recv).start()

            @pl.when(d != me)
            def _():
                pltpu.make_async_remote_copy(
                    back.at[:, d], block_of(out, me), back_send, back_recv,
                    device_id=(d, sub), device_id_type=MESH,
                ).start()

    amounts(jnp.where(first == 0, mixed[0], jnp.where(first == 1, mixed[1], 0.0)))
    sources(halo_t)
    mixed_edges = halo_copies(halo_t, halo_t.at[:, pl.ds(8, 8)], halo_t.at[:, pl.ds(ROWS, 8)], 2)
    for copy in mixed_edges:
        copy.start()
    for copy in mixed_edges:
        copy.wait()

    @pl.loop(0, ROWS // BLOCK)
    def _(b):
        start = pl.multiple_of(b * BLOCK, BLOCK)
        for m in range(2):
            s = inside(b, halo_t[m, pl.ds(start, BLOCK + 16), :])
            s = s + spread(s)
            extra[m, pl.ds(start, BLOCK), :] = s[8 : BLOCK + 8]

    settle(got.at[:, pl.ds(0, N_MEM - 1)], big_send)
    settle(pix.at[pl.ds(0, N_MEM - 1)], pix_send)
    settle(gram_out.at[pl.ds(0, 15)], gram_send)
    settle(part_in.at[pl.ds(0, 15)], part_send)
    settle(full.at[pl.ds(0, 15)], full_send)
    settle(back.at[:, pl.ds(0, N_MEM - 1)], back_send)
    settle(out, back_recv)

    @pl.loop(0, ROWS // BLOCK)
    def _(b):
        here = pl.ds(pl.multiple_of(b * BLOCK, BLOCK), BLOCK)
        for m in range(2):
            out[m, here, :] += extra[m, here, :]


def body(prior, share, cells, steps, pixel, kelvin, weight):
    vmem, any_space = pl.BlockSpec(memory_space=pltpu.VMEM), pl.BlockSpec(memory_space=pl.ANY)
    dma = pltpu.SemaphoreType.DMA
    shape = jax.ShapeDtypeStruct((2, ROWS, COLS), F32)
    n = 2 * N_MEM
    return pl.pallas_call(
        kernel,
        out_shape=shape,
        in_specs=[any_space, pl.BlockSpec(memory_space=pltpu.SMEM)] + [any_space] * 5,
        out_specs=vmem,
        scratch_shapes=[
            pltpu.VMEM((2, ROWS, COLS), F32),
            pltpu.VMEM((SEG, RAYS), I32),
            pltpu.VMEM((1, RAYS), I32),
            pltpu.VMEM((N_MEM, PIX), I32),
            pltpu.VMEM((1, PIX), F32),
            pltpu.VMEM((1, PIX), F32),
            pltpu.VMEM((2, ROWS + 16, COLS), F32),
            pltpu.VMEM((2, ROWS + 16, COLS), F32),
            pltpu.VMEM((2, ROWS + 16, COLS), F32),
            pltpu.VMEM((2, ROWS, COLS), F32),
            pltpu.VMEM((SEG * RAYS, COLS), BF16),
            pltpu.VMEM((4 * ROWS, SEG * RAYS), BF16),
            pltpu.VMEM((N_MEM, 2, PIX), F32),
            pltpu.VMEM((N_MEM, 2, PIX), F32),
            pltpu.VMEM((16, 8, 256), F32),
            pltpu.VMEM((16, 8, 256), F32),
            pltpu.VMEM((16, 8, 256), F32),
            pltpu.VMEM((16, 8, 256), F32),
            pltpu.VMEM((2, N_MEM, 8, 512), F32),
            pltpu.VMEM((8 * n, 512), BF16),
            pltpu.VMEM((8 * n, 512), BF16),
            pltpu.VMEM((n, 8 * n), BF16),
            pltpu.VMEM((n, 8 * n), BF16),
            pltpu.VMEM((2, N_MEM, 8, 512), F32),
            dma,
            dma((5,)),
            dma((2, 3)),
            dma((2, 3)),
        ]
        + [dma] * 12,
        compiler_params=pltpu.CompilerParams(
            collective_id=0, has_side_effects=True, vmem_limit_bytes=57 * 2**20
        ),
    )(prior, share, cells[0].T, steps, pixel[0], kelvin[0], weight[0])


def solution(mesh):
    placed = (
        P("mem", "sub", None),
        P("mem"),
        P("sub", None, None),
        P("sub", None),
        P("sub", None, None),
        P("sub", "mem", None),
        P("sub", "mem", None),
    )
    return jax.shard_map(
        body, mesh=mesh, in_specs=placed, out_specs=P("mem", "sub", None), check_vma=False
    )
```

```python
import functools
import math

import jax
import jax.numpy as jnp
from jax import lax
from jax.experimental import pallas as pl
from jax.experimental.pallas import tpu as pltpu
from jax.sharding import PartitionSpec as P

MESH = pl.DeviceIdType.MESH
HIGHEST = lax.Precision.HIGHEST
ITERS = 20
CONDUCT = 0.2
F32, BF16, I32 = jnp.float32, jnp.bfloat16, jnp.int32
N_MEM, N_SUB = 64, 4
ROWS, COLS = 256, 1024
SEG, RAYS = 32, 64
PIX = 128
BLOCK = 32
INNER = 24
STEP = 27
FIRST = 12
BATCHES = (24, 36, 38, 48, 56, 64)


def dot(a, b, precision=None):
    return jnp.dot(a, b, preferred_element_type=F32, precision=precision)


def iota(shape, dim):
    return lax.broadcasted_iota(I32, shape, dim)


def split(x):
    hi = x.astype(BF16)
    return hi, (x - hi.astype(F32)).astype(BF16)


def fades(share, shape):
    k = iota(shape, 1)
    base = jnp.broadcast_to(1.0 - share, shape)
    out = jnp.broadcast_to(share, shape)
    for bit in range(5):
        out = jnp.where(((k >> bit) & 1) == 1, out * base, out)
        base = base * base
    return out


def spread(v):
    col = iota(v.shape, 1)
    n = v.shape[0]
    left = jnp.where(col == 0, 0.0, pltpu.roll(v, 1, 1))
    right = jnp.where(col == COLS - 1, 0.0, pltpu.roll(v, COLS - 1, 1))
    return CONDUCT * (v + pltpu.roll(v, 1, 0) + pltpu.roll(v, n - 1, 0) + left + right)


def kernel(
    prior, whole, real,
    out,
    extra, field, halo_s, halo_t, flown, onehot, amount,
    pix, pix_in, gram_out, gram_in, part_in, full,
    got, got_hi, got_lo, grid_hi, grid_lo, mix_hi, mix_lo, back,
    load_sem, up_sem, down_sem, big_send, big_recv, pix_send, pix_recv,
    gram_send, gram_recv, part_send, part_recv, full_send, full_recv, back_send, back_recv,
):
    me, sub = lax.axis_index("mem"), lax.axis_index("sub")
    y, zc = me // 16, lax.rem(me, 16)
    q = y * N_SUB + sub

    def plane_peer(i):
        return lax.rem(me + i, N_MEM)

    def xy_peer(p):
        return ((p // N_SUB) * 16 + zc, lax.rem(p, N_SUB))

    def zc_peer(p):
        return (y * 16 + p, sub)

    above = (me, lax.rem(sub + N_SUB - 1, N_SUB))
    below = (me, lax.rem(sub + 1, N_SUB))

    barrier = pltpu.get_barrier_semaphore()

    @pl.loop(1, N_MEM)
    def _(i):
        pl.semaphore_signal(barrier, inc=1, device_id=(plane_peer(i), sub), device_id_type=MESH)

    @pl.loop(1, 16)
    def _(i):
        pl.semaphore_signal(barrier, inc=1, device_id=xy_peer(lax.rem(q + i, 16)), device_id_type=MESH)

    load = pltpu.make_async_copy(prior, field.at[:, pl.ds(8, ROWS)], load_sem)
    load.start()
    pl.semaphore_wait(barrier, N_MEM - 1 + 15)

    def halo_copies(ref, top, bottom, slot):
        return (
            pltpu.make_async_remote_copy(
                top, ref.at[:, pl.ds(ROWS + 8, 8)], up_sem.at[0, slot], up_sem.at[1, slot],
                device_id=above, device_id_type=MESH,
            ),
            pltpu.make_async_remote_copy(
                bottom, ref.at[:, pl.ds(0, 8)], down_sem.at[0, slot], down_sem.at[1, slot],
                device_id=below, device_id_type=MESH,
            ),
        )

    edges = halo_copies(field, prior.at[:, pl.ds(0, 8)], prior.at[:, pl.ds(ROWS - 8, 8)], 0)
    for copy in edges:
        copy.start()

    def inside(b, v):
        row = sub * ROWS + b * BLOCK - 8 + iota(v.shape, 0)
        return jnp.where((row >= 0) & (row < N_SUB * ROWS), v, 0.0)

    load.wait()

    @pl.loop(0, (ROWS - 16) // INNER)
    def _(b):
        start = pl.multiple_of(8 + b * INNER, 8)
        for m in range(2):
            v = spread(spread(field[m, pl.ds(start, INNER + 16), :]))
            flown[m, pl.ds(start, INNER), :] = v[8 : INNER + 8]

    def block_of(ref, d):
        return ref.at[
            :, pl.ds(pl.multiple_of((d // 2) * 8, 8), 8),
            pl.ds(pl.multiple_of(lax.rem(d, 2) * 512, 512), 512),
        ]

    def send_block(d):
        pltpu.make_async_remote_copy(
            block_of(flown, d), got.at[:, me], big_send, big_recv,
            device_id=(d, sub), device_id_type=MESH,
        ).start()

    def target(k):
        return plane_peer(lax.rem(k * STEP, N_MEM))

    def send_big(low, high):
        @pl.loop(low, high)
        def _(k):
            send_block(target(k))

    @pl.loop(1, FIRST)
    def _(k):
        d = target(k)

        @pl.when((d >= 2) & (d < N_MEM - 2))
        def _():
            send_block(d)

    for copy in edges:
        copy.wait()
    for start in (0, ROWS - 8):
        row = sub * ROWS + start - 8 + iota((24, COLS), 0)
        inner = (row >= 0) & (row < N_SUB * ROWS)
        for m in range(2):
            v = jnp.where(inner, field[m, start : start + 24, :], 0.0)
            v = spread(jnp.where(inner, spread(v), 0.0))
            flown[m, start : start + 8, :] = v[8:16]

    keep = pltpu.make_async_copy(block_of(flown, me), got.at[:, me], big_recv)
    keep.start()
    @pl.loop(1, FIRST)
    def _(k):
        d = target(k)

        @pl.when((d < 2) | (d >= N_MEM - 2))
        def _():
            send_block(d)

    send_big(FIRST, BATCHES[0])

    cells = whole[N_MEM : N_MEM + SEG, :RAYS]
    steps = whole[N_MEM + SEG : N_MEM + SEG + 8, :][0:1, :RAYS]
    kelvin, weight = real[0:1, :], real[1:2, :]
    share = real[2:3, 0:1], real[2:3, 1:2]

    lanes = iota((RAYS, COLS), 1)
    upright = jnp.transpose(cells)
    for k in range(SEG):
        col = upright[:, k : k + 1] & (COLS - 1)
        onehot[k * RAYS : (k + 1) * RAYS, :] = jnp.where(lanes == col, 1.0, 0.0).astype(BF16)

    quad = [
        jnp.concatenate([cells[4 * c + i : 4 * c + i + 1, :] for i in range(4)], axis=1)
        for c in range(8)
    ]
    live_steps = jnp.concatenate([steps] * 4, axis=1)

    def amounts(fade8):
        for c in range(8):
            step = iota((SEG, 256), 1) // RAYS + 4 * c
            grown = jnp.where(iota((SEG, 256), 0) == step, 1.0, 0.0)
            value = dot(fade8, grown, HIGHEST)
            value = jnp.where(step[:1] < live_steps, value, 0.0)
            hit = iota((ROWS, 256), 0) == (quad[c] >> 10)
            for m in range(2):
                row = value[m : m + 1, :]
                hi = row.astype(BF16).astype(F32)
                for part, piece in enumerate((hi, row - hi)):
                    top = (2 * part + m) * ROWS
                    amount[top : top + ROWS, c * 256 : (c + 1) * 256] = jnp.where(
                        hit, piece, 0.0
                    ).astype(BF16)

    def sources(into):
        @pl.loop(0, 4)
        def _(t):
            here = pl.ds(pl.multiple_of(t * 256, 256), 256)
            total = dot(amount[...], onehot[:, here])
            total = total[: 2 * ROWS] + total[2 * ROWS :]
            for m in range(2):
                into[m, pl.ds(8, ROWS), here] = total[m * ROWS : (m + 1) * ROWS]

    first = iota((8, SEG), 0)
    own = jnp.where(first == 0, share[0], share[1])
    amounts(fades(own, (8, SEG)))

    sources(halo_s)
    source_edges = halo_copies(halo_s, halo_s.at[:, pl.ds(8, 8)], halo_s.at[:, pl.ds(ROWS, 8)], 1)
    for copy in source_edges:
        copy.start()

    for copy in source_edges:
        copy.wait()

    sides = iota((8, PIX), 0)

    @pl.loop(0, ROWS // BLOCK)
    def _(b):
        start = pl.multiple_of(b * BLOCK, BLOCK)
        forecast = []
        for m in range(2):
            s = inside(b, halo_s[m, pl.ds(start, BLOCK + 16), :])
            s = s + spread(s)
            forecast.append(flown[m, pl.ds(start, BLOCK), :] + s[8 : BLOCK + 8])
        for t in range(BLOCK // 8):
            j = b * (BLOCK // 4) + 2 * t
            cell = jnp.where(sides < 4, whole[pl.ds(j, 1), :], whole[pl.ds(j + 1, 1), :])
            lane, part, row = cell & 127, (cell >> 7) & 7, cell >> 10
            for m in range(2):
                tile = forecast[m][8 * t : 8 * t + 8]
                found = jnp.zeros((8, PIX), F32)
                for w in range(8):
                    picked = jnp.take_along_axis(tile[:, w * 128 : (w + 1) * 128], lane, axis=1)
                    found = jnp.where(part == w, picked, found)
                found = jnp.where((sides & 3) == row, found, 0.0)
                pix[j, m : m + 1, :] = jnp.sum(found[0:4], axis=0, keepdims=True)
                pix[j + 1, m : m + 1, :] = jnp.sum(found[4:8], axis=0, keepdims=True)

    @pl.loop(1, N_MEM)
    def _(i):
        d = plane_peer(i)
        pltpu.make_async_remote_copy(
            pix.at[d], pix_in.at[me], pix_send, pix_recv, device_id=(d, sub), device_id_type=MESH
        ).start()

    send_big(BATCHES[0], BATCHES[1])
    pix_in[me] = pix[me]

    def settle(view, sem):
        pltpu.make_async_copy(view, view, sem).wait()

    settle(pix_in.at[pl.ds(0, N_MEM - 1)], pix_recv)

    seen = jnp.concatenate([pix_in[:, 0, :], pix_in[:, 1, :]], axis=0)
    average = jnp.sum(seen, axis=0, keepdims=True) / (2 * N_MEM)
    seen = seen - average
    misfit = jnp.where(iota((PIX, PIX), 0) == 0, kelvin - average, 0.0)
    both = jnp.concatenate([seen, misfit], axis=0)
    gram = lax.dot_general(
        seen * weight, both, (((1,), (1,)), ((), ())),
        preferred_element_type=F32, precision=HIGHEST,
    )
    row, col = iota((2 * N_MEM, 256), 0), iota((2 * N_MEM, 256), 1)
    carried = jnp.where(row == me, share[0], jnp.where(row == N_MEM + me, share[1], 0.0))
    gram = jnp.where((col == 129) & (sub == 0), carried, gram)
    gram_out[...] = gram.reshape(16, 8, 256)

    def to_peers(count_from, source, target, send, recv, peer):
        @pl.loop(1, 16)
        def _(i):
            p = lax.rem(count_from + i, 16)
            pltpu.make_async_remote_copy(
                source(p), target, send, recv, device_id=peer(p), device_id_type=MESH
            ).start()

    to_peers(q, lambda p: gram_out.at[p], gram_in.at[q], gram_send, gram_recv, xy_peer)
    send_big(BATCHES[1], BATCHES[2])
    gram_in[q] = gram_out[q]
    settle(gram_in.at[pl.ds(0, 15)], gram_recv)
    part_in[zc] = jnp.sum(gram_in[...], axis=0)
    to_peers(zc, lambda p: part_in.at[zc], part_in.at[zc], part_send, part_recv, zc_peer)
    send_big(BATCHES[2], BATCHES[3])
    settle(part_in.at[pl.ds(0, 15)], part_recv)
    full[q] = jnp.sum(part_in[...], axis=0)
    to_peers(q, lambda p: full.at[q], full.at[q], full_send, full_recv, xy_peer)
    send_big(BATCHES[3], BATCHES[4])
    settle(full.at[pl.ds(0, 15)], full_recv)
    send_big(BATCHES[4], BATCHES[5])

    n = 2 * N_MEM
    total = full[...].reshape(n, 256)
    eye = jnp.where(iota((n, n), 0) == iota((n, n), 1), 1.0, 0.0)
    system = (n - 1.0) * eye + total[:, :n]
    norm = jnp.sqrt(jnp.sum(system * system, axis=(0, 1), keepdims=True))

    def parts(x):
        a = x.astype(BF16)
        x = x - a.astype(F32)
        b = x.astype(BF16)
        return a, b, (x - b.astype(F32)).astype(BF16)

    def dot6(x, y):
        (a, b, c), (d, e, f) = x, y
        left = jnp.concatenate([a, a], axis=1), jnp.concatenate([b, a], axis=1), jnp.concatenate([c, b], axis=1)
        right = jnp.concatenate([d, e], axis=0), jnp.concatenate([d, f], axis=0)
        return dot(left[0], right[0]) + (dot(left[1], right[1]) + dot(left[2], right[0]))

    def newton(_, pair):
        u, v = parts(pair[0]), parts(pair[1])
        s = parts(1.5 * eye - 0.5 * dot6(v, u))
        return dot6(u, s), dot6(s, v)

    _, v = lax.fori_loop(0, ITERS, newton, (system / norm, eye))
    root = v / jnp.sqrt(norm)
    shift = dot(root, dot(root, total[:, n:], HIGHEST), HIGHEST)[:, :1]
    transform = math.sqrt(n - 1.0) * root + shift

    fade = fades(total[:, n + 1 : n + 2], (n, SEG))
    fade_mean = jnp.sum(fade, axis=0, keepdims=True) / n
    fade = fade - fade_mean
    mixed = []
    for m in range(2):
        column = jnp.where(iota((n, n), 1) == m * N_MEM + me, transform, 0.0)
        column = jnp.sum(column, axis=1, keepdims=True)
        mixed.append(fade_mean + jnp.sum(column * fade, axis=0, keepdims=True))

    grow = jnp.where(iota((n, 8 * n), 0) == iota((n, 8 * n), 1) // 8, 1.0, 0.0).astype(BF16)
    turned_hi, turned_lo = split(jnp.transpose(transform))
    grid_lo[...] = grow
    grid_hi[...] = dot(turned_hi, grid_lo[...]).astype(BF16)
    grid_lo[...] = dot(turned_lo, grid_lo[...]).astype(BF16)

    same_row = lax.rem(iota((n, 8 * n), 0), 8) == lax.rem(iota((n, 8 * n), 1), 8)

    def expand(turn):
        c = lax.rem(me // 8 + turn, 8)
        r, k = iota((n, n), 0), iota((n, n), 1)
        pick = (r // N_MEM) * N_MEM + 8 * c + lax.rem(r, N_MEM) // 8 == k
        pick = jnp.where(pick, 1.0, 0.0).astype(BF16)
        mix_hi[...] = jnp.where(same_row, dot(pick, grid_hi[...]), 0.0).astype(BF16)
        mix_lo[...] = jnp.where(same_row, dot(pick, grid_lo[...]), 0.0).astype(BF16)

    expand(0)
    settle(got, big_recv)
    mean = jnp.sum(got[...], axis=(0, 1)) / n
    mean2 = jnp.concatenate([mean, mean], axis=0)

    @pl.loop(0, N_MEM, unroll=4)
    def _(i):
        m, s = i // (N_MEM // 2), lax.rem(i, N_MEM // 2)
        pert = got[m, pl.ds(2 * s, 2)].reshape(16, 512) - mean2
        hi, lo = split(pert)
        here = pl.ds(pl.multiple_of(i * 16, 16), 16)
        got_hi[here, :] = hi
        got_lo[here, :] = lo

    @pl.loop(0, 8)
    def _(turn):
        c = lax.rem(me // 8 + turn, 8)
        hi, lo = mix_hi[...], mix_lo[...]
        new = dot(hi, got_hi[...]) + (dot(hi, got_lo[...]) + dot(lo, got_hi[...]))
        new = new.reshape(2, 8, 8, 512) + mean
        back[:, pl.ds(8 * c, 8)] = new

        @pl.loop(0, 8)
        def _(i):
            d = 8 * c + lax.rem(me + i, 8)

            @pl.when(d == me)
            def _():
                pltpu.make_async_copy(back.at[:, d], block_of(out, me), back_recv).start()

            @pl.when(d != me)
            def _():
                pltpu.make_async_remote_copy(
                    back.at[:, d], block_of(out, me), back_send, back_recv,
                    device_id=(d, sub), device_id_type=MESH,
                ).start()

        expand(turn + 1)

    amounts(jnp.where(first == 0, mixed[0], jnp.where(first == 1, mixed[1], 0.0)))
    sources(halo_t)
    mixed_edges = halo_copies(halo_t, halo_t.at[:, pl.ds(8, 8)], halo_t.at[:, pl.ds(ROWS, 8)], 2)
    for copy in mixed_edges:
        copy.start()
    for copy in mixed_edges:
        copy.wait()

    @pl.loop(0, ROWS // BLOCK)
    def _(b):
        start = pl.multiple_of(b * BLOCK, BLOCK)
        for m in range(2):
            s = inside(b, halo_t[m, pl.ds(start, BLOCK + 16), :])
            s = s + spread(s)
            extra[m, pl.ds(start, BLOCK), :] = s[8 : BLOCK + 8]

    settle(got.at[:, pl.ds(0, N_MEM - 1)], big_send)
    settle(pix.at[pl.ds(0, N_MEM - 1)], pix_send)
    settle(gram_out.at[pl.ds(0, 15)], gram_send)
    settle(part_in.at[pl.ds(0, 15)], part_send)
    settle(full.at[pl.ds(0, 15)], full_send)
    settle(back.at[:, pl.ds(0, N_MEM - 1)], back_send)
    settle(out, back_recv)

    @pl.loop(0, ROWS // BLOCK)
    def _(b):
        here = pl.ds(pl.multiple_of(b * BLOCK, BLOCK), BLOCK)
        for m in range(2):
            out[m, here, :] += extra[m, here, :]


def body(prior, share, cells, steps, pixel, kelvin, weight):
    vmem, any_space = pl.BlockSpec(memory_space=pltpu.VMEM), pl.BlockSpec(memory_space=pl.ANY)
    dma = pltpu.SemaphoreType.DMA
    shape = jax.ShapeDtypeStruct((2, ROWS, COLS), F32)
    n = 2 * N_MEM

    def stack(pieces, rows):
        total, top = 0, 0
        for x in pieces:
            below = rows - top - x.shape[0]
            total += jnp.pad(x, ((top, below), (0, PIX - x.shape[1])))
            top += x.shape[0]
        return total

    whole = stack((pixel[0], cells[0].T, steps), N_MEM + SEG + 8)
    real = stack((kelvin[0], weight[0], share[None]), 8)
    return pl.pallas_call(
        kernel,
        out_shape=shape,
        in_specs=[any_space, vmem, vmem],
        out_specs=vmem,
        scratch_shapes=[
            pltpu.VMEM((2, ROWS, COLS), F32),
            pltpu.VMEM((2, ROWS + 16, COLS), F32),
            pltpu.VMEM((2, ROWS + 16, COLS), F32),
            pltpu.VMEM((2, ROWS + 16, COLS), F32),
            pltpu.VMEM((2, ROWS, COLS), F32),
            pltpu.VMEM((SEG * RAYS, COLS), BF16),
            pltpu.VMEM((4 * ROWS, SEG * RAYS), BF16),
            pltpu.VMEM((N_MEM, 2, PIX), F32),
            pltpu.VMEM((N_MEM, 2, PIX), F32),
            pltpu.VMEM((16, 8, 256), F32),
            pltpu.VMEM((16, 8, 256), F32),
            pltpu.VMEM((16, 8, 256), F32),
            pltpu.VMEM((16, 8, 256), F32),
            pltpu.VMEM((2, N_MEM, 8, 512), F32),
            pltpu.VMEM((8 * n, 512), BF16),
            pltpu.VMEM((8 * n, 512), BF16),
            pltpu.VMEM((n, 8 * n), BF16),
            pltpu.VMEM((n, 8 * n), BF16),
            pltpu.VMEM((n, 8 * n), BF16),
            pltpu.VMEM((n, 8 * n), BF16),
            pltpu.VMEM((2, N_MEM, 8, 512), F32),
            dma,
            dma((2, 3)),
            dma((2, 3)),
        ]
        + [dma] * 12,
        compiler_params=pltpu.CompilerParams(
            collective_id=0, has_side_effects=True, vmem_limit_bytes=50 * 2**20
        ),
    )(prior, whole, real)


def solution(mesh):
    placed = (
        P("mem", "sub", None),
        P("mem"),
        P("sub", None, None),
        P("sub", None),
        P("sub", None, None),
        P("sub", "mem", None),
        P("sub", "mem", None),
    )
    return jax.shard_map(
        body, mesh=mesh, in_specs=placed, out_specs=P("mem", "sub", None), check_vma=False
    )
```

```python
import functools
import math

import jax
import jax.numpy as jnp
from jax import lax
from jax.experimental import pallas as pl
from jax.experimental.pallas import tpu as pltpu
from jax.sharding import PartitionSpec as P

MESH = pl.DeviceIdType.MESH
HIGHEST = lax.Precision.HIGHEST
ITERS = 20
CONDUCT = 0.2
F32, BF16, I32 = jnp.float32, jnp.bfloat16, jnp.int32
N_MEM, N_SUB = 64, 4
ROWS, COLS = 256, 1024
SEG, RAYS = 32, 64
PIX = 128
BLOCK = 32
INNER = 24
STEP = 27
FIRST = 12
BATCHES = (24, 36, 38, 48, 56, 64)


def dot(a, b, precision=None):
    return jnp.dot(a, b, preferred_element_type=F32, precision=precision)


def iota(shape, dim):
    return lax.broadcasted_iota(I32, shape, dim)


def split(x):
    hi = x.astype(BF16)
    return hi, (x - hi.astype(F32)).astype(BF16)


def fades(share, shape):
    k = iota(shape, 1)
    base = jnp.broadcast_to(1.0 - share, shape)
    out = jnp.broadcast_to(share, shape)
    for bit in range(5):
        out = jnp.where(((k >> bit) & 1) == 1, out * base, out)
        base = base * base
    return out


def spread(v):
    col = iota(v.shape, 1)
    n = v.shape[0]
    left = jnp.where(col == 0, 0.0, pltpu.roll(v, 1, 1))
    right = jnp.where(col == COLS - 1, 0.0, pltpu.roll(v, COLS - 1, 1))
    return CONDUCT * (v + pltpu.roll(v, 1, 0) + pltpu.roll(v, n - 1, 0) + left + right)


def kernel(
    prior, whole, real,
    out,
    extra, field, halo_s, halo_t, flown, onehot, amount,
    pix, pix_in, gram_out, gram_in, part_in, full,
    got, got_hi, got_lo, grid_hi, grid_lo, mix_hi, mix_lo, back,
    load_sem, up_sem, down_sem, big_send, big_recv, pix_send, pix_recv,
    gram_send, gram_recv, part_send, part_recv, full_send, full_recv, back_send, back_recv,
):
    me, sub = lax.axis_index("mem"), lax.axis_index("sub")
    y, zc = me // 16, lax.rem(me, 16)
    q = y * N_SUB + sub

    def plane_peer(i):
        return lax.rem(me + i, N_MEM)

    def xy_peer(p):
        return ((p // N_SUB) * 16 + zc, lax.rem(p, N_SUB))

    def zc_peer(p):
        return (y * 16 + p, sub)

    above = (me, lax.rem(sub + N_SUB - 1, N_SUB))
    below = (me, lax.rem(sub + 1, N_SUB))

    barrier = pltpu.get_barrier_semaphore()

    @pl.loop(1, N_MEM)
    def _(i):
        pl.semaphore_signal(barrier, inc=1, device_id=(plane_peer(i), sub), device_id_type=MESH)

    @pl.loop(1, 16)
    def _(i):
        pl.semaphore_signal(barrier, inc=1, device_id=xy_peer(lax.rem(q + i, 16)), device_id_type=MESH)

    load = pltpu.make_async_copy(prior, field.at[:, pl.ds(8, ROWS)], load_sem)
    load.start()
    pl.semaphore_wait(barrier, N_MEM - 1 + 15)

    def halo_copies(ref, top, bottom, slot):
        return (
            pltpu.make_async_remote_copy(
                top, ref.at[:, pl.ds(ROWS + 8, 8)], up_sem.at[0, slot], up_sem.at[1, slot],
                device_id=above, device_id_type=MESH,
            ),
            pltpu.make_async_remote_copy(
                bottom, ref.at[:, pl.ds(0, 8)], down_sem.at[0, slot], down_sem.at[1, slot],
                device_id=below, device_id_type=MESH,
            ),
        )

    edges = halo_copies(field, prior.at[:, pl.ds(0, 8)], prior.at[:, pl.ds(ROWS - 8, 8)], 0)
    for copy in edges:
        copy.start()

    def inside(b, v):
        row = sub * ROWS + b * BLOCK - 8 + iota(v.shape, 0)
        return jnp.where((row >= 0) & (row < N_SUB * ROWS), v, 0.0)

    load.wait()

    @pl.loop(0, (ROWS - 16) // INNER)
    def _(b):
        start = pl.multiple_of(8 + b * INNER, 8)
        for m in range(2):
            v = spread(spread(field[m, pl.ds(start, INNER + 16), :]))
            flown[m, pl.ds(start, INNER), :] = v[8 : INNER + 8]

    def block_of(ref, d):
        return ref.at[
            :, pl.ds(pl.multiple_of((d // 2) * 8, 8), 8),
            pl.ds(pl.multiple_of(lax.rem(d, 2) * 512, 512), 512),
        ]

    def send_block(d):
        pltpu.make_async_remote_copy(
            block_of(flown, d), got.at[:, me], big_send, big_recv,
            device_id=(d, sub), device_id_type=MESH,
        ).start()

    def target(k):
        return plane_peer(lax.rem(k * STEP, N_MEM))

    def send_big(low, high):
        @pl.loop(low, high)
        def _(k):
            send_block(target(k))

    @pl.loop(1, FIRST)
    def _(k):
        d = target(k)

        @pl.when((d >= 2) & (d < N_MEM - 2))
        def _():
            send_block(d)

    for copy in edges:
        copy.wait()
    for start in (0, ROWS - 8):
        row = sub * ROWS + start - 8 + iota((24, COLS), 0)
        inner = (row >= 0) & (row < N_SUB * ROWS)
        for m in range(2):
            v = jnp.where(inner, field[m, start : start + 24, :], 0.0)
            v = spread(jnp.where(inner, spread(v), 0.0))
            flown[m, start : start + 8, :] = v[8:16]

    keep = pltpu.make_async_copy(block_of(flown, me), got.at[:, me], big_recv)
    keep.start()
    @pl.loop(1, FIRST)
    def _(k):
        d = target(k)

        @pl.when((d < 2) | (d >= N_MEM - 2))
        def _():
            send_block(d)

    send_big(FIRST, BATCHES[0])

    cells = whole[N_MEM : N_MEM + SEG, :RAYS]
    steps = whole[N_MEM + SEG : N_MEM + SEG + 8, :][0:1, :RAYS]
    kelvin, weight = real[0:1, :], real[1:2, :]
    share = real[2:3, 0:1], real[2:3, 1:2]

    lanes = iota((RAYS, COLS), 1)
    upright = jnp.transpose(cells)
    for k in range(SEG):
        col = upright[:, k : k + 1] & (COLS - 1)
        onehot[k * RAYS : (k + 1) * RAYS, :] = jnp.where(lanes == col, 1.0, 0.0).astype(BF16)

    quad = [
        jnp.concatenate([cells[4 * c + i : 4 * c + i + 1, :] for i in range(4)], axis=1)
        for c in range(8)
    ]
    live_steps = jnp.concatenate([steps] * 4, axis=1)

    def amounts(fade8):
        for c in range(8):
            step = iota((SEG, 256), 1) // RAYS + 4 * c
            grown = jnp.where(iota((SEG, 256), 0) == step, 1.0, 0.0)
            value = dot(fade8, grown, HIGHEST)
            value = jnp.where(step[:1] < live_steps, value, 0.0)
            hit = iota((ROWS, 256), 0) == (quad[c] >> 10)
            for m in range(2):
                row = value[m : m + 1, :]
                hi = row.astype(BF16).astype(F32)
                for part, piece in enumerate((hi, row - hi)):
                    top = (2 * part + m) * ROWS
                    amount[top : top + ROWS, c * 256 : (c + 1) * 256] = jnp.where(
                        hit, piece, 0.0
                    ).astype(BF16)

    def sources(into):
        @pl.loop(0, 4)
        def _(t):
            here = pl.ds(pl.multiple_of(t * 256, 256), 256)
            total = dot(amount[...], onehot[:, here])
            total = total[: 2 * ROWS] + total[2 * ROWS :]
            for m in range(2):
                into[m, pl.ds(8, ROWS), here] = total[m * ROWS : (m + 1) * ROWS]

    first = iota((8, SEG), 0)
    own = jnp.where(first == 0, share[0], share[1])
    amounts(fades(own, (8, SEG)))

    sources(halo_s)
    source_edges = halo_copies(halo_s, halo_s.at[:, pl.ds(8, 8)], halo_s.at[:, pl.ds(ROWS, 8)], 1)
    for copy in source_edges:
        copy.start()

    for copy in source_edges:
        copy.wait()

    sides = iota((8, PIX), 0)

    @pl.loop(0, ROWS // BLOCK)
    def _(b):
        start = pl.multiple_of(b * BLOCK, BLOCK)
        forecast = []
        for m in range(2):
            s = inside(b, halo_s[m, pl.ds(start, BLOCK + 16), :])
            s = s + spread(s)
            forecast.append(flown[m, pl.ds(start, BLOCK), :] + s[8 : BLOCK + 8])
        for t in range(BLOCK // 8):
            j = b * (BLOCK // 4) + 2 * t
            cell = jnp.where(sides < 4, whole[pl.ds(j, 1), :], whole[pl.ds(j + 1, 1), :])
            lane, part, row = cell & 127, (cell >> 7) & 7, cell >> 10
            for m in range(2):
                tile = forecast[m][8 * t : 8 * t + 8]
                found = jnp.zeros((8, PIX), F32)
                for w in range(8):
                    picked = jnp.take_along_axis(tile[:, w * 128 : (w + 1) * 128], lane, axis=1)
                    found = jnp.where(part == w, picked, found)
                found = jnp.where((sides & 3) == row, found, 0.0)
                pix[j, m : m + 1, :] = jnp.sum(found[0:4], axis=0, keepdims=True)
                pix[j + 1, m : m + 1, :] = jnp.sum(found[4:8], axis=0, keepdims=True)

    @pl.loop(1, N_MEM)
    def _(i):
        d = plane_peer(i)
        pltpu.make_async_remote_copy(
            pix.at[d], pix_in.at[me], pix_send, pix_recv, device_id=(d, sub), device_id_type=MESH
        ).start()

    send_big(BATCHES[0], BATCHES[1])
    pix_in[me] = pix[me]

    def settle(view, sem):
        pltpu.make_async_copy(view, view, sem).wait()

    settle(pix_in.at[pl.ds(0, N_MEM - 1)], pix_recv)

    seen = jnp.concatenate([pix_in[:, 0, :], pix_in[:, 1, :]], axis=0)
    average = jnp.sum(seen, axis=0, keepdims=True) / (2 * N_MEM)
    seen = seen - average
    misfit = jnp.where(iota((PIX, PIX), 0) == 0, kelvin - average, 0.0)
    both = jnp.concatenate([seen, misfit], axis=0)
    gram = lax.dot_general(
        seen * weight, both, (((1,), (1,)), ((), ())),
        preferred_element_type=F32, precision=HIGHEST,
    )
    row, col = iota((2 * N_MEM, 256), 0), iota((2 * N_MEM, 256), 1)
    carried = jnp.where(row == me, share[0], jnp.where(row == N_MEM + me, share[1], 0.0))
    gram = jnp.where((col == 129) & (sub == 0), carried, gram)
    gram_out[...] = gram.reshape(16, 8, 256)

    def to_peers(count_from, source, target, send, recv, peer):
        @pl.loop(1, 16)
        def _(i):
            p = lax.rem(count_from + i, 16)
            pltpu.make_async_remote_copy(
                source(p), target, send, recv, device_id=peer(p), device_id_type=MESH
            ).start()

    to_peers(q, lambda p: gram_out.at[p], gram_in.at[q], gram_send, gram_recv, xy_peer)
    send_big(BATCHES[1], BATCHES[2])
    gram_in[q] = gram_out[q]
    settle(gram_in.at[pl.ds(0, 15)], gram_recv)
    part_in[zc] = jnp.sum(gram_in[...], axis=0)
    to_peers(zc, lambda p: part_in.at[zc], part_in.at[zc], part_send, part_recv, zc_peer)
    send_big(BATCHES[2], BATCHES[3])
    settle(part_in.at[pl.ds(0, 15)], part_recv)
    full[q] = jnp.sum(part_in[...], axis=0)
    to_peers(q, lambda p: full.at[q], full.at[q], full_send, full_recv, xy_peer)
    send_big(BATCHES[3], BATCHES[4])
    settle(full.at[pl.ds(0, 15)], full_recv)
    send_big(BATCHES[4], BATCHES[5])

    n = 2 * N_MEM
    total = full[...].reshape(n, 256)
    eye = jnp.where(iota((n, n), 0) == iota((n, n), 1), 1.0, 0.0)
    system = (n - 1.0) * eye + total[:, :n]
    norm = jnp.sqrt(jnp.sum(system * system, axis=(0, 1), keepdims=True))

    def parts(x):
        a = x.astype(BF16)
        x = x - a.astype(F32)
        b = x.astype(BF16)
        return a, b, (x - b.astype(F32)).astype(BF16)

    def dot6(x, y):
        (a, b, c), (d, e, f) = x, y
        left = jnp.concatenate([a, a], axis=1), jnp.concatenate([b, a], axis=1), jnp.concatenate([c, b], axis=1)
        right = jnp.concatenate([d, e], axis=0), jnp.concatenate([d, f], axis=0)
        return dot(left[0], right[0]) + (dot(left[1], right[1]) + dot(left[2], right[0]))

    def newton(_, pair):
        u, v = parts(pair[0]), parts(pair[1])
        s = parts(1.5 * eye - 0.5 * dot6(v, u))
        return dot6(u, s), dot6(s, v)

    _, v = lax.fori_loop(0, ITERS, newton, (system / norm, eye))
    root = v / jnp.sqrt(norm)
    shift = dot(root, dot(root, total[:, n:], HIGHEST), HIGHEST)[:, :1]
    transform = math.sqrt(n - 1.0) * root + shift

    fade = fades(total[:, n + 1 : n + 2], (n, SEG))
    fade_mean = jnp.sum(fade, axis=0, keepdims=True) / n
    fade = fade - fade_mean
    mixed = []
    for m in range(2):
        column = jnp.where(iota((n, n), 1) == m * N_MEM + me, transform, 0.0)
        column = jnp.sum(column, axis=1, keepdims=True)
        mixed.append(fade_mean + jnp.sum(column * fade, axis=0, keepdims=True))

    grow = jnp.where(iota((n, 8 * n), 0) == iota((n, 8 * n), 1) // 8, 1.0, 0.0).astype(BF16)
    turned_hi, turned_lo = split(jnp.transpose(transform))
    grid_lo[...] = grow
    grid_hi[...] = dot(turned_hi, grid_lo[...]).astype(BF16)
    grid_lo[...] = dot(turned_lo, grid_lo[...]).astype(BF16)

    same_row = lax.rem(iota((n, 8 * n), 0), 8) == lax.rem(iota((n, 8 * n), 1), 8)

    def expand(turn):
        c = lax.rem(me // 8 + turn + 1, 8)
        r, k = iota((n, n), 0), iota((n, n), 1)
        pick = (r // N_MEM) * N_MEM + 8 * c + lax.rem(r, N_MEM) // 8 == k
        pick = jnp.where(pick, 1.0, 0.0).astype(BF16)
        mix_hi[...] = jnp.where(same_row, dot(pick, grid_hi[...]), 0.0).astype(BF16)
        mix_lo[...] = jnp.where(same_row, dot(pick, grid_lo[...]), 0.0).astype(BF16)

    expand(0)
    settle(got, big_recv)
    mean = jnp.sum(got[...], axis=(0, 1)) / n
    mean2 = jnp.concatenate([mean, mean], axis=0)

    @pl.loop(0, N_MEM, unroll=4)
    def _(i):
        m, s = i // (N_MEM // 2), lax.rem(i, N_MEM // 2)
        pert = got[m, pl.ds(2 * s, 2)].reshape(16, 512) - mean2
        hi, lo = split(pert)
        here = pl.ds(pl.multiple_of(i * 16, 16), 16)
        got_hi[here, :] = hi
        got_lo[here, :] = lo

    @pl.loop(0, 8)
    def _(turn):
        c = lax.rem(me // 8 + turn + 1, 8)
        hi, lo = mix_hi[...], mix_lo[...]
        new = dot(hi, got_hi[...]) + (dot(hi, got_lo[...]) + dot(lo, got_hi[...]))
        new = new.reshape(2, 8, 8, 512) + mean
        back[:, pl.ds(8 * c, 8)] = new

        @pl.loop(0, 8)
        def _(i):
            d = 8 * c + lax.rem(me + i, 8)

            @pl.when(d == me)
            def _():
                pltpu.make_async_copy(back.at[:, d], block_of(out, me), back_recv).start()

            @pl.when(d != me)
            def _():
                pltpu.make_async_remote_copy(
                    back.at[:, d], block_of(out, me), back_send, back_recv,
                    device_id=(d, sub), device_id_type=MESH,
                ).start()

        expand(turn + 1)

    amounts(jnp.where(first == 0, mixed[0], jnp.where(first == 1, mixed[1], 0.0)))
    sources(halo_t)
    mixed_edges = halo_copies(halo_t, halo_t.at[:, pl.ds(8, 8)], halo_t.at[:, pl.ds(ROWS, 8)], 2)
    for copy in mixed_edges:
        copy.start()
    for copy in mixed_edges:
        copy.wait()

    @pl.loop(0, ROWS // BLOCK)
    def _(b):
        start = pl.multiple_of(b * BLOCK, BLOCK)
        for m in range(2):
            s = inside(b, halo_t[m, pl.ds(start, BLOCK + 16), :])
            s = s + spread(s)
            extra[m, pl.ds(start, BLOCK), :] = s[8 : BLOCK + 8]

    settle(got.at[:, pl.ds(0, N_MEM - 1)], big_send)
    settle(pix.at[pl.ds(0, N_MEM - 1)], pix_send)
    settle(gram_out.at[pl.ds(0, 15)], gram_send)
    settle(part_in.at[pl.ds(0, 15)], part_send)
    settle(full.at[pl.ds(0, 15)], full_send)
    settle(back.at[:, pl.ds(0, N_MEM - 1)], back_send)
    settle(out, back_recv)

    @pl.loop(0, ROWS // BLOCK)
    def _(b):
        here = pl.ds(pl.multiple_of(b * BLOCK, BLOCK), BLOCK)
        for m in range(2):
            out[m, here, :] += extra[m, here, :]


def body(prior, share, cells, steps, pixel, kelvin, weight):
    vmem, any_space = pl.BlockSpec(memory_space=pltpu.VMEM), pl.BlockSpec(memory_space=pl.ANY)
    dma = pltpu.SemaphoreType.DMA
    shape = jax.ShapeDtypeStruct((2, ROWS, COLS), F32)
    n = 2 * N_MEM

    def stack(pieces, rows):
        total, top = 0, 0
        for x in pieces:
            below = rows - top - x.shape[0]
            total += jnp.pad(x, ((top, below), (0, PIX - x.shape[1])))
            top += x.shape[0]
        return total

    whole = stack((pixel[0], cells[0].T, steps), N_MEM + SEG + 8)
    real = stack((kelvin[0], weight[0], share[None]), 8)
    return pl.pallas_call(
        kernel,
        out_shape=shape,
        in_specs=[any_space, vmem, vmem],
        out_specs=vmem,
        scratch_shapes=[
            pltpu.VMEM((2, ROWS, COLS), F32),
            pltpu.VMEM((2, ROWS + 16, COLS), F32),
            pltpu.VMEM((2, ROWS + 16, COLS), F32),
            pltpu.VMEM((2, ROWS + 16, COLS), F32),
            pltpu.VMEM((2, ROWS, COLS), F32),
            pltpu.VMEM((SEG * RAYS, COLS), BF16),
            pltpu.VMEM((4 * ROWS, SEG * RAYS), BF16),
            pltpu.VMEM((N_MEM, 2, PIX), F32),
            pltpu.VMEM((N_MEM, 2, PIX), F32),
            pltpu.VMEM((16, 8, 256), F32),
            pltpu.VMEM((16, 8, 256), F32),
            pltpu.VMEM((16, 8, 256), F32),
            pltpu.VMEM((16, 8, 256), F32),
            pltpu.VMEM((2, N_MEM, 8, 512), F32),
            pltpu.VMEM((8 * n, 512), BF16),
            pltpu.VMEM((8 * n, 512), BF16),
            pltpu.VMEM((n, 8 * n), BF16),
            pltpu.VMEM((n, 8 * n), BF16),
            pltpu.VMEM((n, 8 * n), BF16),
            pltpu.VMEM((n, 8 * n), BF16),
            pltpu.VMEM((2, N_MEM, 8, 512), F32),
            dma,
            dma((2, 3)),
            dma((2, 3)),
        ]
        + [dma] * 12,
        compiler_params=pltpu.CompilerParams(
            collective_id=0, has_side_effects=True, vmem_limit_bytes=50 * 2**20
        ),
    )(prior, whole, real)


def solution(mesh):
    placed = (
        P("mem", "sub", None),
        P("mem"),
        P("sub", None, None),
        P("sub", None),
        P("sub", None, None),
        P("sub", "mem", None),
        P("sub", "mem", None),
    )
    return jax.shard_map(
        body, mesh=mesh, in_specs=placed, out_specs=P("mem", "sub", None), check_vma=False
    )
```
